1024 devices in a mesh: grp: 16 (over y, core), gx: 64 (over x, z).
Axes of the slice: x: 4, y: 8, z: 16, core: 2. Of those that a mesh axis runs over, the one named last changes fastest.
Arguments:
- voltages: bfloat16 [16, 512, 2, 1, 2, 16384], P('grp', 'gx'), may hold values from -6 to 6
- tile_of: int32 [16, 32768], P(None, 'gx'), may hold values from -1 to 15, as said below
- cell_of: int32 [16, 32768], P(None, 'gx'), may hold values from 0 to 127
Outputs:
- image: float32 [16, 2, 4096, 4096], P('grp', None, 'gx')
The draws below stay inside these ranges and needn't reach their ends.
Inputs may be any that keep to these rules, and one draw needn't show every extreme that they name: `tile_of`: among the 512 blocks of one coarse channel and one gx index, no tile is named more than 8 times, and one tile exactly 8 times; -1 marks blocks that no tile takes.
All inputs are finite; a program needn't handle non-finite values.
Results may differ from the reference program's by a relative error of at most 0.006.
Values may be sent and summed in bfloat16 or wider, within the bound.
A program may use at most 64 MiB of HBM per device.

```python
import jax
import jax.numpy as jnp
from jax import lax

NFINE = 16384
AVG = 256
ST = 512
POL = 2
NSPEC = 1
NIN = 1024
BR = 16
BC = 128
TILE = 4096
COARSE = 16
OUT_DEV = 1
NB = 512
NBLK = 32768
CAP = 8
SLAB = 64
CELLS = 128
N_GRP = 16
N_GX = 64


def draw_tile_of(key, part):
    keys = jax.random.split(key, COARSE * N_GX)

    def one_row(row_key):
        first, second, third = jax.random.split(row_key, 3)
        tiles = jnp.arange(N_GRP, dtype=jnp.int32)
        busiest = jax.random.randint(first, (), 0, N_GRP, dtype=jnp.int32)
        lower = jax.random.randint(second, (N_GRP,), 1, CAP // 2 + 1, dtype=jnp.int32)
        counts = jnp.where(tiles == busiest, CAP, lower).astype(jnp.int32)
        ends = jnp.cumsum(counts).astype(jnp.int32)
        position = jnp.arange(NB, dtype=jnp.int32)
        tile_at = jnp.sum((position[:, None] >= ends[None, :]).astype(jnp.int32), axis=1)
        tile_at = jnp.where(tile_at >= N_GRP, -1, tile_at).astype(jnp.int32)
        order = jax.random.permutation(third, NB).astype(jnp.int32)
        return jnp.zeros((NB,), jnp.int32).at[order].set(tile_at)
    rows = jax.vmap(one_row)(keys)
    return rows.reshape(COARSE, N_GX * NB).astype(jnp.int32)


def touch_ends(result, own_key, smallest, largest):
    dims = result.shape
    index_at = [jax.random.randint(jax.random.fold_in(own_key, axis), (), 0, dims[axis]) for axis in range(len(dims))]
    result = result.at[tuple(index_at)].set(smallest)
    longest = dims.index(max(dims))
    index_at[longest] = (index_at[longest] + 1) % dims[longest]
    return result.at[tuple(index_at)].set(largest)


def steps_of(key, extent, pieces, low, top_value):
    def one(dim, blocks):
        draws = jax.random.uniform(jax.random.fold_in(jax.random.fold_in(key, 6), dim), (blocks,), jnp.float32, low / len(pieces), top_value / len(pieces))
        return jnp.repeat(jnp.exp(draws), extent[dim] // blocks).reshape((-1,) + (1,) * (len(extent) - dim - 1))

    factor_of = one(*pieces[0])
    for cut in pieces[1:]:
        factor_of = factor_of * one(*cut)
    return factor_of


def centred(stream_key, extent, scale, most, cuts=(), kind=jnp.bfloat16):
    values = jax.random.normal(stream_key, extent, jnp.float32) * scale
    if len(cuts) > 0:
        values = steps_of(stream_key, extent, cuts, -0.22, 0.18) * values
    return jnp.clip(values, min=-most, max=most).astype(kind)


def setup_inputs(seed: int = 0) -> dict:
    splits = jax.random.split(jax.random.key(seed), 4)
    return {
        "voltages": centred(splits[0], (COARSE, ST, POL, NSPEC, 2, NFINE), 1.0, 6.0, ((0, 16), (1, 64))),
        "tile_of": draw_tile_of(jax.random.fold_in(splits[3], 71), 0),
        "cell_of": touch_ends(jax.random.randint(splits[2], (COARSE, NBLK), 0, CELLS), jax.random.fold_in(splits[2], 1), 0, CELLS - 1).astype(jnp.int32),
    }


def spectra_of(volt):
    field = volt[:, :, :, 0].astype(jnp.float32) + 1j * volt[:, :, :, 1].astype(jnp.float32)
    spec = jnp.fft.fft(field, axis=-1, norm="ortho")
    return jnp.stack([jnp.real(spec), jnp.imag(spec)], axis=3).astype(jnp.bfloat16)


def blocks_of(spec):
    nout = NFINE // AVG
    grouped = spec.reshape(NIN, NSPEC, 2, nout, AVG).astype(jnp.float32)
    gram = jnp.einsum("psrof,qsxof->orpxq", grouped, grouped, precision=lax.Precision.HIGHEST)
    factor = 1.0 / (NSPEC * AVG) ** 0.5
    vis_re = (gram[:, 0, :, 0, :] + gram[:, 1, :, 1, :]) * factor
    vis_im = (gram[:, 1, :, 0, :] - gram[:, 0, :, 1, :]) * factor
    vis = jnp.stack([vis_re, vis_im], axis=1).astype(jnp.bfloat16)
    shaped = vis.reshape(N_GX, OUT_DEV, 2, NIN // BR, BR, NIN // BC, BC)
    return shaped.transpose(0, 1, 3, 5, 2, 4, 6).reshape(N_GX * NB, 2 * BR * BC)


def reference(voltages, tile_of, cell_of):
    total_cells = N_GRP * N_GX * CELLS

    def add_group(grid, inputs):
        volt, tiles, cells = inputs
        blocks = blocks_of(spectra_of(volt)).astype(jnp.float32)
        owner = jnp.arange(N_GX * NB, dtype=jnp.int32) // NB
        ids = ((tiles * N_GX + owner) * CELLS + cells).astype(jnp.int32)
        ids = jnp.where(tiles < 0, total_cells, ids).astype(jnp.int32)
        return grid.at[ids].add(blocks, mode="drop"), None

    start = jnp.zeros((total_cells, 2 * BR * BC), jnp.float32)
    grid, _ = lax.scan(add_group, start, (voltages, tile_of, cell_of))
    grid = grid.reshape(N_GRP, N_GX * CELLS, 2 * BR * BC)

    def image_of(cells_grid):
        field = cells_grid.reshape(N_GX, SLAB // BR, TILE // BC, 2, BR, BC)
        field = field.transpose(3, 0, 1, 4, 2, 5).reshape(2, TILE, TILE)
        rows = jnp.fft.ifft(field[0] + 1j * field[1], axis=1, norm="ortho")
        rows_re = lax.optimization_barrier(jnp.real(rows).astype(jnp.bfloat16)).astype(jnp.float32)
        rows_im = lax.optimization_barrier(jnp.imag(rows).astype(jnp.bfloat16)).astype(jnp.float32)
        cols = jnp.fft.ifft(rows_re + 1j * rows_im, axis=0, norm="ortho")
        return jnp.stack([jnp.real(cols).T, jnp.imag(cols).T]).astype(jnp.float32)

    return lax.map(image_of, grid)
```

```python
import functools
import math

import jax
import jax.numpy as jnp
import numpy as np
from jax import lax
from jax.experimental import pallas as pl
from jax.experimental.pallas import tpu as pltpu
from jax.sharding import PartitionSpec as P

F32 = jnp.float32
BF16 = jnp.bfloat16
MESH = pl.DeviceIdType.MESH
VMEM_LIMIT = 56 * 1024 * 1024


def split(table):
    high = table.astype(np.float32).astype(jnp.bfloat16)
    low = (table - high.astype(np.float64)).astype(np.float32).astype(jnp.bfloat16)
    return high, low


def turn(left, right, size, sign):
    angle = sign * 2.0 * math.pi / size * (np.outer(left, right) % size)
    return np.cos(angle), np.sin(angle)


@functools.cache
def tables():
    made = {}
    i128 = np.arange(128)
    c, s = turn(i128, i128, 128, -1)
    m1 = np.zeros((2, 128, 128, 2))
    m1[0, :, :, 0], m1[0, :, :, 1] = c, -s
    m1[1, :, :, 0], m1[1, :, :, 1] = s, c
    made["m1"] = np.concatenate(split(m1.reshape(256, 256)))
    made["tw1"] = np.stack(turn(i128, i128, 16384, -1)).astype(np.float32)
    c, s = turn(i128, i128, 128, -1)
    c, s = (t.reshape(64, 2, 128).transpose(1, 0, 2).reshape(128, 128) / 128.0 for t in (c, s))
    made["v1"] = np.concatenate(split(np.block([[c, -s], [s, c]])))
    c, s = turn(np.arange(32), np.arange(32), 32, 1)
    w = np.zeros((2, 4, 32, 2, 4, 32))
    for rb in range(4):
        w[0, rb, :, 0, rb], w[0, rb, :, 1, rb] = c, -s
        w[1, rb, :, 0, rb], w[1, rb, :, 1, rb] = s, c
    made["w"] = np.concatenate(split(w.reshape(256, 256)))
    tw = np.stack(turn(np.arange(32), i128, 4096, 1))
    made["tw2"] = np.tile(tw, (1, 4, 1)).astype(np.float32)
    c, s = turn(i128, i128, 128, 1)
    c, s = (t.reshape(64, 2, 128).transpose(1, 0, 2).reshape(128, 128) / 64.0 for t in (c, s))
    made["v2"] = np.concatenate(split(np.block([[c, -s], [s, c]])))
    n1 = (2 * np.arange(64)[None, :] + np.arange(2)[:, None]).reshape(128)
    c, s = turn(n1, i128, 128, 1)
    made["m4"] = np.concatenate(split(np.block([[c, s], [-s, c]])), axis=1)
    n0 = np.arange(32)
    tw = np.stack(turn(n0, i128, 4096, 1)).reshape(2, 2, 16, 1, 128)
    made["tw4"] = np.broadcast_to(tw, (2, 2, 16, 8, 128)).reshape(2, 2, 128, 128).astype(np.float32)
    c, s = turn(n0, n0, 32, 1)
    v4 = np.block([[c, -s], [s, c]]) / 64.0
    made["v4"] = np.concatenate(split(np.kron(v4, np.eye(8))))
    return made


def nt(left, right):
    return lax.dot_general(left, right, (((1,), (1,)), ((), ())), preferred_element_type=F32)


def tn(left, right):
    return lax.dot_general(left, right, (((0,), (0,)), ((), ())), preferred_element_type=F32)


def nn(left, right):
    return jnp.dot(left, right, preferred_element_type=F32)


def route_kernel(tile_ref, cell_ref, w_ref, idx_ref, place_ref):
    me = lax.axis_index("grp")
    tiles = tile_ref[...]
    mine = tile_ref[pl.ds(me, 1), :]
    marks = jnp.concatenate(
        [mine == lax.broadcasted_iota(jnp.int32, (16, 512), 0), tiles == me], axis=0
    ).astype(F32)
    before = lax.broadcasted_iota(jnp.int32, (512, 512), 0) < lax.broadcasted_iota(
        jnp.int32, (512, 512), 1
    )
    rank = nn(marks.astype(BF16), before.astype(F32).astype(BF16))
    rank = jnp.where(marks > 0.5, rank, -1.0).astype(jnp.int32)
    position = lax.broadcasted_iota(jnp.int32, (16, 512), 1)
    columns = [
        jnp.sum(jnp.where(rank[:16] == k, position, 0), axis=1, keepdims=True) for k in range(8)
    ]
    idx_ref[...] = jnp.concatenate(columns, axis=1)
    slot = lax.broadcasted_iota(jnp.int32, (8, 512), 0)
    lane = lax.broadcasted_iota(jnp.int32, (8, 256), 1)
    hits = []
    for g in range(16):
        chosen = rank[16 + g : 17 + g] == slot
        cell = jnp.sum(jnp.where(chosen, cell_ref[g : g + 1, :] + 1, 0), axis=1, keepdims=True) - 1
        for part in range(2):
            at = jnp.where(cell < 0, -1, cell + 128 * part)
            hits.append((lane == at).astype(F32))
    onehot = jnp.concatenate(hits, axis=0).astype(BF16)
    place_ref[...] = nt(w_ref[...], onehot).astype(BF16)


def partner(me, step):
    dx = lax.rem(step, 4)
    d = step // 4
    up = (d + 1) // 2
    dz = jnp.where(lax.rem(d, 2) == 1, up, 16 - up)
    x, z = me // 16, lax.rem(me, 16)
    to = lax.rem(x + dx, 4) * 16 + lax.rem(z + dz, 16)
    source = lax.rem(x + 4 - dx, 4) * 16 + lax.rem(z + 16 - lax.rem(dz, 16), 16)
    return to, source


def greet_gx(me):
    barrier = pltpu.get_barrier_semaphore()

    def hello(step, carry):
        to, _ = partner(me, step)
        pl.semaphore_signal(barrier, inc=1, device_id={"gx": to}, device_id_type=MESH)
        return carry

    lax.fori_loop(1, 64, hello, 0)


def gx_copy(send_ref, recv_ref, send_sem, recv_sem, to, slot):
    return pltpu.make_async_remote_copy(
        src_ref=send_ref.at[to],
        dst_ref=recv_ref.at[slot],
        send_sem=send_sem.at[to],
        recv_sem=recv_sem.at[slot],
        device_id={"gx": to},
        device_id_type=MESH,
    )


def spectra_phase(x_ref, m1_ref, tw_ref, v_ref, z_ref):
    def pair(h, carry):
        x = jnp.concatenate([x_ref[2 * h], x_ref[2 * h + 1]], axis=1)
        y = nn(m1_ref[...], x)
        y = y[:256] + y[256:]
        for o in range(2):
            q = 2 * h + o
            re, im = y[:128, o * 128 : o * 128 + 128], y[128:, o * 128 : o * 128 + 128]
            cos, sin = tw_ref[0], tw_ref[1]
            both = jnp.concatenate([re * cos - im * sin, re * sin + im * cos], axis=1)
            high = both.astype(BF16)
            low = (both - high.astype(F32)).astype(BF16)
            out = nt(v_ref[...], high)
            out = out[:256] + out[256:] + nt(v_ref[:256], low)
            for s in range(4):
                z_ref[pl.ds(s * 16 + q, 64, stride=64), :] = out[s * 64 : s * 64 + 64]
        return carry

    lax.fori_loop(0, 8, pair, 0)


def operand(recv_ref, at):
    return jnp.concatenate(
        [recv_ref[pl.ds(at * 16, 16), s * 16 : s * 16 + 16, :].reshape(256, 128) for s in range(4)],
        axis=1,
    )


def gram_phase(recv_ref, vis_ref):
    def column(p, carry):
        right = operand(recv_ref, p)
        crossed = jnp.concatenate([-right[:, 256:], right[:, :256]], axis=1)

        def row(r, inner):
            left = operand(recv_ref, r)
            for part, other in enumerate((right, crossed)):
                out = nt(left, other)
                for half in range(2):
                    vis_ref[pl.ds(r * 16, 16), 2 * p + half, part * 16 : part * 16 + 16, :] = out[
                        :, half * 128 : half * 128 + 128
                    ].reshape(16, 16, 128)
            return inner

        lax.fori_loop(0, 4, row, 0)
        return carry

    lax.fori_loop(0, 4, column, 0)


def gather_phase(idx_ref, vis_ref, o_ref, out_ref):
    def tile(t, carry):
        for k in range(8):
            b = idx_ref[t, k]
            block = vis_ref[b // 8, b % 8]
            for part in range(2):
                o_ref[pl.ds(t * 256 + part * 8 + k, 16, stride=16), :] = block[
                    part * 16 : part * 16 + 16
                ]
        out_ref[t] = (o_ref[pl.ds(t * 256, 256), :] * 0.0625).astype(BF16)
        return carry

    lax.fori_loop(0, 16, tile, 0)


def correlate_kernel(
    x_ref, m1_ref, tw_ref, v_ref, idx_ref, out_ref, z_ref, vis_ref, send_ref, recv_ref, send_sem, recv_sem
):
    me = lax.axis_index("gx")
    greet_gx(me)
    spectra_phase(x_ref, m1_ref, tw_ref, v_ref, z_ref)
    pl.semaphore_wait(pltpu.get_barrier_semaphore(), 63)

    def push(step, carry):
        to, _ = partner(me, step)
        send_ref[to] = z_ref[pl.ds(pl.multiple_of(to * 64, 64), 64), :].astype(BF16)
        gx_copy(send_ref, recv_ref, send_sem, recv_sem, to, me).start()
        return carry

    lax.fori_loop(1, 64, push, 0)
    recv_ref[me] = z_ref[pl.ds(pl.multiple_of(me * 64, 64), 64), :].astype(BF16)

    def take(step, carry):
        to, source = partner(me, step)
        gx_copy(send_ref, recv_ref, send_sem, recv_sem, to, source).wait()
        return carry

    lax.fori_loop(1, 64, take, 0)
    gram_phase(recv_ref, vis_ref)
    gather_phase(idx_ref, vis_ref, z_ref, out_ref)


def rows_phase(got_ref, place_ref, tw_ref, v_ref, y_ref, z_ref):
    def line(i, carry):
        block = got_ref[:, pl.ds(pl.multiple_of(i * 16, 16), 16), :].reshape(256, 128)
        y = nn(place_ref[...], block)
        y = y[:256] + y[256:]
        re, im = y[:128], y[128:]
        cos, sin = tw_ref[0], tw_ref[1]
        at = pl.ds(pl.multiple_of(i * 8, 8), 8)
        y_ref[:, at, 0:128] = (re * cos - im * sin).reshape(16, 8, 128)
        y_ref[:, at, 128:256] = (re * sin + im * cos).reshape(16, 8, 128)
        return carry

    lax.fori_loop(0, 16, line, 0, unroll=2)

    def second(m, carry):
        out = nt(v_ref[...], y_ref[m].astype(BF16))
        out = out[:256] + out[256:]
        for s in range(4):
            z_ref[pl.ds(m * 4 + s, 64, stride=64), :] = out[s * 64 : s * 64 + 64]
        return carry

    lax.fori_loop(0, 16, second, 0, unroll=2)


def rows_kernel(
    blocks_ref, place_ref, tw_ref, v_ref, out_ref,
    got_ref, y_ref, z_ref, x_ref, send_ref, recv_ref, bsend_sem, brecv_sem, send_sem, recv_sem,
):
    me = lax.axis_index("gx")
    grp = lax.axis_index("grp")
    barrier = pltpu.get_barrier_semaphore()

    def hello(step, carry):
        to = lax.rem(grp + step, 16)
        pl.semaphore_signal(barrier, inc=1, device_id={"grp": to}, device_id_type=MESH)
        return carry

    lax.fori_loop(1, 16, hello, 0)
    greet_gx(me)
    pl.semaphore_wait(barrier, 78)

    def block_copy(to, slot):
        return pltpu.make_async_remote_copy(
            src_ref=blocks_ref.at[to],
            dst_ref=got_ref.at[slot],
            send_sem=bsend_sem.at[to],
            recv_sem=brecv_sem.at[slot],
            device_id={"grp": to},
            device_id_type=MESH,
        )

    def push_blocks(step, carry):
        block_copy(lax.rem(grp + step, 16), grp).start()
        return carry

    lax.fori_loop(1, 16, push_blocks, 0)
    got_ref[grp] = blocks_ref[grp]

    def take_blocks(step, carry):
        block_copy(lax.rem(grp + step, 16), lax.rem(grp + 16 - step, 16)).wait()
        return carry

    lax.fori_loop(1, 16, take_blocks, 0)
    rows_phase(got_ref, place_ref, tw_ref, v_ref, y_ref, z_ref)

    def push(step, carry):
        to, _ = partner(me, step)
        send_ref[to] = z_ref[pl.ds(pl.multiple_of(to * 64, 64), 64), :].astype(BF16)
        gx_copy(send_ref, recv_ref, send_sem, recv_sem, to, me).start()
        return carry

    lax.fori_loop(1, 64, push, 0)
    own = z_ref[pl.ds(pl.multiple_of(me * 64, 64), 64), :].astype(BF16)
    x_ref[pl.ds(me, 64, stride=64), :] = own.astype(F32)

    def take(step, carry):
        to, source = partner(me, step)
        gx_copy(send_ref, recv_ref, send_sem, recv_sem, to, source).wait()
        x_ref[pl.ds(source, 64, stride=64), :] = recv_ref[source].astype(F32)
        return carry

    lax.fori_loop(1, 64, take, 0)
    out_ref[...] = x_ref[...].astype(BF16)


def columns_kernel(x_ref, m4_ref, tw_ref, v_ref, image_ref):
    def eight(h, carry):
        k2, k1 = h // 4, h % 4
        turned = []
        for n in range(2):
            x = jnp.concatenate(
                [
                    x_ref[(2 * bit + n) * 16 + k1 * 4 + part * 2 + k2]
                    for part in range(2)
                    for bit in range(2)
                ],
                axis=0,
            )
            t = tn(x, m4_ref[...])
            t = t[:, :256] + t[:, 256:]
            re, im = t[:, :128], t[:, 128:]
            cos, sin = tw_ref[0, n], tw_ref[1, n]
            turned.append((re * cos - im * sin, re * sin + im * cos))
        t = jnp.concatenate([turned[0][0], turned[1][0], turned[0][1], turned[1][1]], axis=0)
        out = nn(v_ref[...], t.astype(BF16))
        out = out[:512] + out[512:]
        for part in range(2):
            for k in range(32):
                image_ref[part, pl.ds(pl.multiple_of(h * 8, 8), 8), k * 128 : k * 128 + 128] = out[
                    (part * 32 + k) * 8 : (part * 32 + k) * 8 + 8
                ]
        return carry

    lax.fori_loop(0, 8, eight, 0)


def params(**more):
    return pltpu.CompilerParams(vmem_limit_bytes=VMEM_LIMIT, **more)


def on_device(voltages, tile_of, cell_of):
    tab = {name: jnp.asarray(value) for name, value in tables().items()}
    vmem = pl.BlockSpec(memory_space=pltpu.VMEM)
    smem = pl.BlockSpec(memory_space=pltpu.SMEM)
    idx, place = pl.pallas_call(
        route_kernel,
        out_shape=(
            jax.ShapeDtypeStruct((16, 8), jnp.int32),
            jax.ShapeDtypeStruct((512, 256), BF16),
        ),
        compiler_params=params(),
        name="route",
    )(tile_of, cell_of, tab["w"])
    volts = voltages.reshape(16, 2, 128, 128).transpose(0, 2, 1, 3).reshape(16, 256, 128)
    blocks = pl.pallas_call(
        correlate_kernel,
        out_shape=jax.ShapeDtypeStruct((16, 256, 128), BF16),
        in_specs=[vmem] * 4 + [smem],
        out_specs=vmem,
        scratch_shapes=[
            pltpu.VMEM((4096, 128), F32),
            pltpu.VMEM((64, 8, 32, 128), F32),
            pltpu.VMEM((64, 64, 128), BF16),
            pltpu.VMEM((64, 64, 128), BF16),
            pltpu.SemaphoreType.DMA((64,)),
            pltpu.SemaphoreType.DMA((64,)),
        ],
        compiler_params=params(collective_id=0, has_side_effects=True),
        name="correlate",
    )(volts, tab["m1"], tab["tw1"], tab["v1"], idx)
    columns = pl.pallas_call(
        rows_kernel,
        out_shape=jax.ShapeDtypeStruct((4096, 128), BF16),
        in_specs=[vmem] * 4,
        out_specs=vmem,
        scratch_shapes=[
            pltpu.VMEM((16, 256, 128), BF16),
            pltpu.VMEM((16, 128, 256), F32),
            pltpu.VMEM((4096, 128), F32),
            pltpu.VMEM((4096, 128), F32),
            pltpu.VMEM((64, 64, 128), BF16),
            pltpu.VMEM((64, 64, 128), BF16),
            pltpu.SemaphoreType.DMA((16,)),
            pltpu.SemaphoreType.DMA((16,)),
            pltpu.SemaphoreType.DMA((64,)),
            pltpu.SemaphoreType.DMA((64,)),
        ],
        compiler_params=params(collective_id=1, has_side_effects=True),
        name="rows",
    )(blocks, place, tab["tw2"], tab["v2"])
    image = pl.pallas_call(
        columns_kernel,
        out_shape=jax.ShapeDtypeStruct((2, 64, 4096), F32),
        in_specs=[vmem] * 4,
        out_specs=vmem,
        compiler_params=params(),
        name="columns",
    )(columns.reshape(64, 64, 128), tab["m4"], tab["tw4"], tab["v4"])
    return image.reshape(1, 2, 64, 4096)


def solution(mesh):
    in_specs = (P("grp", "gx", None, None, None, None), P(None, "gx"), P(None, "gx"))
    out_specs = P("grp", None, "gx", None)
    return jax.shard_map(
        on_device, mesh=mesh, in_specs=in_specs, out_specs=out_specs, check_vma=False
    )
```

```python
import functools
import math

import jax
import jax.numpy as jnp
import numpy as np
from jax import lax
from jax.experimental import pallas as pl
from jax.experimental.pallas import tpu as pltpu
from jax.sharding import PartitionSpec as P

F32 = jnp.float32
BF16 = jnp.bfloat16
MESH = pl.DeviceIdType.MESH


def split(table):
    high = table.astype(np.float32).astype(jnp.bfloat16)
    low = (table - high.astype(np.float64)).astype(np.float32).astype(jnp.bfloat16)
    return high, low


def turn(left, right, size, sign):
    angle = sign * 2.0 * math.pi / size * (np.outer(left, right) % size)
    return np.cos(angle), np.sin(angle)


@functools.cache
def tables():
    made = {}
    i128 = np.arange(128)
    c, s = turn(i128, i128, 128, -1)
    m1 = np.zeros((2, 128, 128, 2))
    m1[0, :, :, 0], m1[0, :, :, 1] = c, -s
    m1[1, :, :, 0], m1[1, :, :, 1] = s, c
    made["m1"] = np.concatenate(split(m1.reshape(256, 256)))
    made["tw1"] = np.stack(turn(i128, i128, 16384, -1)).astype(np.float32)
    c, s = turn(i128, i128, 128, -1)
    c, s = (t.reshape(64, 2, 128).transpose(1, 0, 2).reshape(128, 128) / 128.0 for t in (c, s))
    made["v1"] = np.concatenate(split(np.block([[c, -s], [s, c]])))
    c, s = turn(np.arange(32), np.arange(32), 32, 1)
    w = np.zeros((2, 4, 32, 2, 4, 32))
    for rb in range(4):
        w[0, rb, :, 0, rb], w[0, rb, :, 1, rb] = c, -s
        w[1, rb, :, 0, rb], w[1, rb, :, 1, rb] = s, c
    made["w"] = np.concatenate(split(w.reshape(256, 256)))
    tw = np.stack(turn(np.arange(32), i128, 4096, 1))
    made["tw2"] = np.tile(tw, (1, 4, 1)).astype(np.float32)
    c, s = turn(i128, i128, 128, 1)
    c, s = (t.reshape(64, 2, 128).transpose(1, 0, 2).reshape(128, 128) / 64.0 for t in (c, s))
    made["v2"] = np.concatenate(split(np.block([[c, -s], [s, c]])))
    n1 = (2 * np.arange(64)[None, :] + np.arange(2)[:, None]).reshape(128)
    c, s = turn(n1, i128, 128, 1)
    made["m4"] = np.concatenate(split(np.block([[c, s], [-s, c]])), axis=1)
    n0 = np.arange(32)
    tw = np.stack(turn(n0, i128, 4096, 1)).reshape(2, 4, 8, 1, 128)
    made["tw4"] = np.broadcast_to(tw, (2, 4, 8, 16, 128)).reshape(2, 4, 128, 128).astype(np.float32)
    c, s = turn(n0, n0, 32, 1)
    v4 = np.block([[c, -s], [s, c]]) / 64.0
    made["v4"] = np.concatenate(split(np.kron(v4, np.eye(8))))
    return made


def nt(left, right):
    return lax.dot_general(left, right, (((1,), (1,)), ((), ())), preferred_element_type=F32)


def tn(left, right):
    return lax.dot_general(left, right, (((0,), (0,)), ((), ())), preferred_element_type=F32)


def nn(left, right):
    return jnp.dot(left, right, preferred_element_type=F32)


def route_phase(me, tile_ref, cell_ref, w_ref, idx_ref, place_ref):
    tiles = tile_ref[...]
    mine = tile_ref[pl.ds(me, 1), :]
    marks = jnp.concatenate(
        [mine == lax.broadcasted_iota(jnp.int32, (16, 512), 0), tiles == me], axis=0
    ).astype(F32)
    before = lax.broadcasted_iota(jnp.int32, (512, 512), 0) < lax.broadcasted_iota(
        jnp.int32, (512, 512), 1
    )
    rank = nn(marks.astype(BF16), before.astype(F32).astype(BF16))
    rank = jnp.where(marks > 0.5, rank, -1.0).astype(jnp.int32)
    position = lax.broadcasted_iota(jnp.int32, (16, 512), 1)
    columns = [
        jnp.sum(jnp.where(rank[:16] == k, position, 0), axis=1, keepdims=True) for k in range(8)
    ]
    idx_ref[...] = jnp.concatenate(columns + [columns[0]] * 120, axis=1)
    slot = lax.broadcasted_iota(jnp.int32, (8, 512), 0)
    lane = lax.broadcasted_iota(jnp.int32, (8, 256), 1)
    hits = []
    for g in range(16):
        chosen = rank[16 + g : 17 + g] == slot
        cell = jnp.sum(jnp.where(chosen, cell_ref[g : g + 1, :] + 1, 0), axis=1, keepdims=True) - 1
        for part in range(2):
            at = jnp.where(cell < 0, -1, cell + 128 * part)
            hits.append((lane == at).astype(F32))
    onehot = jnp.concatenate(hits, axis=0).astype(BF16)
    place_ref[...] = nt(w_ref[...], onehot).astype(BF16)


def partner(me, dx, d):
    up = (d + 1) // 2
    dz = jnp.where(lax.rem(d, 2) == 1, up, lax.rem(16 - up, 16))
    x, z = me // 16, lax.rem(me, 16)
    to = lax.rem(x + dx, 4) * 16 + lax.rem(z + dz, 16)
    source = lax.rem(x + 4 - dx, 4) * 16 + lax.rem(z + 16 - dz, 16)
    return to, source


def by_row(me, step):
    return partner(me, step // 16, lax.rem(step, 16))


def by_distance(me, step):
    return partner(me, lax.rem(step, 4), step // 4)


def gx_copy(send_ref, recv_ref, send_sem, recv_sem, to, slot):
    return pltpu.make_async_remote_copy(
        src_ref=send_ref.at[to],
        dst_ref=recv_ref.at[slot],
        send_sem=send_sem.at[to],
        recv_sem=recv_sem.at[slot],
        device_id={"gx": to},
        device_id_type=MESH,
    )


def grp_copy(send_ref, recv_ref, send_sem, recv_sem, to, slot):
    return pltpu.make_async_remote_copy(
        src_ref=send_ref.at[to],
        dst_ref=recv_ref.at[slot],
        send_sem=send_sem.at[to],
        recv_sem=recv_sem.at[slot],
        device_id={"grp": to},
        device_id_type=MESH,
    )


def greet(me, grp):
    barrier = pltpu.get_barrier_semaphore()

    def along_gx(step, carry):
        to, _ = by_row(me, step)
        pl.semaphore_signal(barrier, inc=1, device_id={"gx": to}, device_id_type=MESH)
        return carry

    lax.fori_loop(1, 64, along_gx, 0)

    def along_grp(step, carry):
        to = lax.rem(grp + step, 16)
        pl.semaphore_signal(barrier, inc=1, device_id={"grp": to}, device_id_type=MESH)
        return carry

    lax.fori_loop(1, 16, along_grp, 0)


def spectra_phase(x_ref, m1_ref, tw_ref, v_ref, z_ref):
    def pair(h, carry):
        x = jnp.concatenate([x_ref[2 * h], x_ref[2 * h + 1]], axis=1)
        y = nn(m1_ref[...], x)
        y = y[:256] + y[256:]
        cos, sin = tw_ref[0], tw_ref[1]
        both = []
        for o in range(2):
            re, im = y[:128, o * 128 : o * 128 + 128], y[128:, o * 128 : o * 128 + 128]
            both.append(jnp.concatenate([re * cos - im * sin, re * sin + im * cos], axis=1))
        both = jnp.concatenate(both, axis=0)
        high = both.astype(BF16)
        low = (both - high.astype(F32)).astype(BF16)
        out = nt(v_ref[...], high)
        out = out[:256] + out[256:] + nt(v_ref[:256], low)
        for o in range(2):
            for s in range(4):
                z_ref[pl.ds(s * 16 + 2 * h + o, 64, stride=64), :] = out[
                    s * 64 : s * 64 + 64, o * 128 : o * 128 + 128
                ]
        return carry

    lax.fori_loop(0, 8, pair, 0)


def operand(recv_ref, at):
    return jnp.concatenate(
        [recv_ref[pl.ds(at * 16, 16), s * 16 : s * 16 + 16, :].reshape(256, 128) for s in range(4)],
        axis=1,
    )


def gram_block(recv_ref, vis_ref, r, p):
    left, right = operand(recv_ref, r), operand(recv_ref, p)
    crossed = jnp.concatenate([-right[:, 256:], right[:, :256]], axis=1)
    for part, other in enumerate((right, crossed)):
        out = nt(left, other)
        for half in range(2):
            vis_ref[pl.ds(r * 16, 16), 2 * p + half, part * 16 : part * 16 + 16, :] = out[
                :, half * 128 : half * 128 + 128
            ].reshape(16, 16, 128)


def gather_phase(h, idx_ref, vis_ref, z_ref, out_ref):
    def tile(t, carry):
        for k in range(8):
            b = idx_ref[t, k]
            block = vis_ref[b // 8, lax.rem(b, 8)]
            for part in range(2):
                z_ref[pl.ds(t * 128 + part * 8 + k, 8, stride=16), :] = block[
                    part * 16 + h * 8 : part * 16 + h * 8 + 8
                ]
        out_ref[t] = (z_ref[pl.ds(t * 128, 128), :] * 0.0625).astype(BF16)
        return carry

    lax.fori_loop(0, 16, tile, 0)


def rows_phase(got_ref, place_ref, tw_ref, v_ref, y_ref, z_ref):
    def line(i, carry):
        block = got_ref[:, pl.ds(pl.multiple_of(i * 16, 16), 16), :].reshape(256, 128)
        y = nn(place_ref[...], block)
        y = y[:256] + y[256:]
        re, im = y[:128], y[128:]
        cos, sin = tw_ref[0], tw_ref[1]
        at = pl.ds(pl.multiple_of(i * 16, 16), 16)
        y_ref[:, at, 0:128] = (re * cos - im * sin).reshape(8, 16, 128)
        y_ref[:, at, 128:256] = (re * sin + im * cos).reshape(8, 16, 128)
        return carry

    lax.fori_loop(0, 8, line, 0, unroll=2)

    def second(m, carry):
        both = jnp.concatenate([y_ref[2 * m], y_ref[2 * m + 1]], axis=0).astype(BF16)
        out = nt(v_ref[...], both)
        if v_ref.shape[0] == 512:
            out = out[:256] + out[256:]
        for o in range(2):
            for s in range(4):
                z_ref[pl.ds((2 * m + o) * 4 + s, 64, stride=32), :] = out[
                    s * 64 : s * 64 + 64, o * 128 : o * 128 + 128
                ]
        return carry

    lax.fori_loop(0, 4, second, 0)


def main_kernel(
    x_ref, tile_ref, cell_ref, m1_ref, tw1_ref, v1_ref, w_ref, tw2_ref, v2_ref, out_ref,
    z_ref, vis_ref, send_ref, recv_ref, idx_ref, pick_ref, place_ref, blocks_ref, got_ref, y_ref, turned_ref,
    rsend_ref, rrecv_ref, send_sem, recv_sem, pick_sem, bsend_sem, brecv_sem, rsend_sem, rrecv_sem,
):
    me, grp = lax.axis_index("gx"), lax.axis_index("grp")
    greet(me, grp)
    spectra_phase(x_ref, m1_ref, tw1_ref, v1_ref, z_ref)
    pl.semaphore_wait(pltpu.get_barrier_semaphore(), 78)

    def push(step, carry):
        to, _ = by_row(me, step)
        send_ref[to] = z_ref[pl.ds(pl.multiple_of(to * 64, 64), 64), :].astype(BF16)
        gx_copy(send_ref, recv_ref, send_sem, recv_sem, to, me).start()
        return carry

    lax.fori_loop(1, 64, push, 0)
    recv_ref[me] = z_ref[pl.ds(pl.multiple_of(me * 64, 64), 64), :].astype(BF16)

    route_phase(grp, tile_ref, cell_ref, w_ref, idx_ref, place_ref)
    picks = pltpu.make_async_copy(idx_ref, pick_ref, pick_sem)
    picks.start()
    picks.wait()

    def take(step, carry):
        to, source = by_row(me, step)
        gx_copy(send_ref, recv_ref, send_sem, recv_sem, to, source).wait()
        return carry

    row = me // 16
    for dx in range(4):
        lax.fori_loop(max(1, 16 * dx), 16 * dx + 16, take, 0)
        new = lax.rem(row + 4 - dx, 4)

        def against(j, carry, new=new):
            gram_block(recv_ref, vis_ref, new, lax.rem(row + 4 - j, 4))
            return carry

        def under(j, carry, new=new):
            gram_block(recv_ref, vis_ref, lax.rem(row + 4 - j, 4), new)
            return carry

        lax.fori_loop(0, dx + 1, against, 0)
        if dx:
            lax.fori_loop(0, dx, under, 0)

    def block_copy(h, to, slot):
        return grp_copy(
            blocks_ref.at[h], got_ref.at[h], bsend_sem.at[h], brecv_sem.at[h], to, slot
        )

    def push_blocks(h):
        def one(step, carry):
            block_copy(h, lax.rem(grp + step, 16), grp).start()
            return carry

        lax.fori_loop(1, 16, one, 0)
        got_ref[h, grp] = blocks_ref[h, grp]

    def take_blocks(h):
        def one(step, carry):
            block_copy(h, lax.rem(grp + step, 16), lax.rem(grp + 16 - step, 16)).wait()
            return carry

        lax.fori_loop(1, 16, one, 0)

    def row_copy(h, to, slot):
        return gx_copy(
            rsend_ref.at[h], rrecv_ref.at[h], rsend_sem.at[h], rrecv_sem.at[h], to, slot
        )

    def push_rows(h):
        def one(step, carry):
            to, _ = by_distance(me, step)
            rsend_ref[h, to] = z_ref[pl.ds(pl.multiple_of(to * 32, 32), 32), :].astype(BF16)
            row_copy(h, to, me).start()
            return carry

        lax.fori_loop(1, 64, one, 0)
        own = z_ref[pl.ds(pl.multiple_of(me * 32, 32), 32), :].astype(BF16)
        turned_ref[pl.ds(h * 2048 + me, 32, stride=64), :] = own.astype(F32)

    def take_rows(h):
        def one(step, carry):
            to, source = by_distance(me, step)
            row_copy(h, to, source).wait()
            turned_ref[pl.ds(h * 2048 + source, 32, stride=64), :] = rrecv_ref[h, source].astype(F32)
            return carry

        lax.fori_loop(1, 64, one, 0)
        out_ref[h * 2048 : h * 2048 + 2048, :] = turned_ref[h * 2048 : h * 2048 + 2048, :].astype(BF16)

    gather_phase(0, pick_ref, vis_ref, z_ref, blocks_ref.at[0])
    push_blocks(0)
    gather_phase(1, pick_ref, vis_ref, z_ref, blocks_ref.at[1])
    take_blocks(0)
    push_blocks(1)
    rows_phase(got_ref.at[0], place_ref, tw2_ref, v2_ref, y_ref, z_ref)
    push_rows(0)
    take_blocks(1)
    rows_phase(got_ref.at[1], place_ref, tw2_ref, v2_ref, y_ref, z_ref)
    push_rows(1)
    take_rows(0)
    take_rows(1)


def columns_kernel(x_ref, m4_ref, tw_ref, v_ref, image_ref):
    e = pl.program_id(0)
    k2, k1 = e // 2, lax.rem(e, 2)
    turned = []
    for n in range(2):
        for h in range(2):
            x = jnp.concatenate(
                [
                    x_ref[h * 32 + (2 * bit + n) * 8 + k1 * 4 + part * 2 + k2]
                    for part in range(2)
                    for bit in range(2)
                ],
                axis=0,
            )
            t = tn(x, m4_ref[...])
            t = t[:, :256] + t[:, 256:]
            re, im = t[:, :128], t[:, 128:]
            cos, sin = tw_ref[0, n * 2 + h], tw_ref[1, n * 2 + h]
            turned.append((re * cos - im * sin, re * sin + im * cos))
    sides = []
    for side in range(2):
        sides.append(
            jnp.concatenate(
                [
                    turned[nh][part].reshape(8, 2, 8, 128)[:, side].reshape(64, 128)
                    for part in range(2)
                    for nh in range(4)
                ],
                axis=0,
            )
        )
    out = nn(v_ref[...], jnp.concatenate(sides, axis=1).astype(BF16))
    if v_ref.shape[0] == 1024:
        out = out[:512] + out[512:]
    for part in range(2):
        for k in range(32):
            for side in range(2):
                image_ref[part, side * 8 : side * 8 + 8, k * 128 : k * 128 + 128] = out[
                    (part * 32 + k) * 8 : (part * 32 + k) * 8 + 8, side * 128 : side * 128 + 128
                ]


def params(mib, **more):
    return pltpu.CompilerParams(vmem_limit_bytes=mib * 1024 * 1024, **more)


def on_device(voltages, tile_of, cell_of):
    tab = {name: jnp.asarray(value) for name, value in tables().items()}
    vmem = pl.BlockSpec(memory_space=pltpu.VMEM)
    volts = voltages.reshape(16, 2, 128, 128).transpose(0, 2, 1, 3).reshape(16, 256, 128)
    columns = pl.pallas_call(
        main_kernel,
        out_shape=jax.ShapeDtypeStruct((4096, 128), BF16),
        in_specs=[vmem] * 9,
        out_specs=vmem,
        scratch_shapes=[
            pltpu.VMEM((4096, 128), F32),
            pltpu.VMEM((64, 8, 32, 128), F32),
            pltpu.VMEM((64, 64, 128), BF16),
            pltpu.VMEM((64, 64, 128), BF16),
            pltpu.VMEM((16, 128), jnp.int32),
            pltpu.SMEM((16, 128), jnp.int32),
            pltpu.VMEM((512, 256), BF16),
            pltpu.VMEM((2, 16, 128, 128), BF16),
            pltpu.VMEM((2, 16, 128, 128), BF16),
            pltpu.VMEM((8, 128, 256), F32),
            pltpu.VMEM((4096, 128), F32),
            pltpu.VMEM((2, 64, 32, 128), BF16),
            pltpu.VMEM((2, 64, 32, 128), BF16),
            pltpu.SemaphoreType.DMA((64,)),
            pltpu.SemaphoreType.DMA((64,)),
            pltpu.SemaphoreType.DMA,
            pltpu.SemaphoreType.DMA((2, 16)),
            pltpu.SemaphoreType.DMA((2, 16)),
            pltpu.SemaphoreType.DMA((2, 64)),
            pltpu.SemaphoreType.DMA((2, 64)),
        ],
        compiler_params=params(40, collective_id=0, has_side_effects=True),
        name="main",
    )(
        volts, tile_of, cell_of, tab["m1"], tab["tw1"], tab["v1"], tab["w"], tab["tw2"], tab["v2"]
    )
    whole = lambda shape: pl.BlockSpec(shape, lambda e: (0,) * len(shape))
    image = pl.pallas_call(
        columns_kernel,
        grid=(4,),
        out_shape=jax.ShapeDtypeStruct((2, 64, 4096), F32),
        in_specs=[whole(s) for s in ((64, 64, 128), tab["m4"].shape, tab["tw4"].shape, tab["v4"].shape)],
        out_specs=pl.BlockSpec((2, 16, 4096), lambda e: (0, e, 0)),
        compiler_params=params(20),
        name="columns",
    )(columns.reshape(64, 64, 128), tab["m4"], tab["tw4"], tab["v4"])
    return image.reshape(1, 2, 64, 4096)


def solution(mesh):
    in_specs = (P("grp", "gx", None, None, None, None), P(None, "gx"), P(None, "gx"))
    out_specs = P("grp", None, "gx", None)
    return jax.shard_map(
        on_device, mesh=mesh, in_specs=in_specs, out_specs=out_specs, check_vma=False
    )
```

```python
import functools
import math

import jax
import jax.numpy as jnp
import numpy as np
from jax import lax
from jax.experimental import pallas as pl
from jax.experimental.pallas import tpu as pltpu
from jax.sharding import PartitionSpec as P

F32 = jnp.float32
BF16 = jnp.bfloat16
MESH = pl.DeviceIdType.MESH


def split(table):
    high = table.astype(np.float32).astype(jnp.bfloat16)
    low = (table - high.astype(np.float64)).astype(np.float32).astype(jnp.bfloat16)
    return high, low


def turn(left, right, size, sign):
    angle = sign * 2.0 * math.pi / size * (np.outer(left, right) % size)
    return np.cos(angle), np.sin(angle)


@functools.cache
def tables():
    made = {}
    i128 = np.arange(128)
    c, s = turn(i128, i128, 128, -1)
    m1 = np.zeros((2, 128, 128, 2))
    m1[0, :, :, 0], m1[0, :, :, 1] = c, -s
    m1[1, :, :, 0], m1[1, :, :, 1] = s, c
    made["m1"] = np.concatenate(split(m1.reshape(256, 256)))
    made["tw1"] = np.stack(turn(i128, i128, 16384, -1)).astype(np.float32)
    c, s = turn(i128, i128, 128, -1)
    c, s = (t.reshape(64, 2, 128).transpose(1, 0, 2).reshape(128, 128) / 128.0 for t in (c, s))
    made["v1"] = np.concatenate(split(np.block([[c, -s], [s, c]])))
    c, s = turn(np.arange(32), np.arange(32), 32, 1)
    w = np.zeros((2, 4, 32, 2, 4, 32))
    for rb in range(4):
        w[0, rb, :, 0, rb], w[0, rb, :, 1, rb] = c, -s
        w[1, rb, :, 0, rb], w[1, rb, :, 1, rb] = s, c
    made["w"] = np.concatenate(split(w.reshape(256, 256)))
    tw = np.stack(turn(np.arange(32), i128, 4096, 1))
    made["tw2"] = np.tile(tw, (1, 4, 1)).astype(np.float32)
    c, s = turn(i128, i128, 128, 1)
    c, s = (t.reshape(64, 2, 128).transpose(1, 0, 2).reshape(128, 128) / 64.0 for t in (c, s))
    made["v2"] = split(np.block([[c, -s], [s, c]]))[0]
    n1 = (2 * np.arange(64)[None, :] + np.arange(2)[:, None]).reshape(128)
    c, s = turn(n1, i128, 128, 1)
    made["m4"] = np.concatenate(split(np.block([[c, s], [-s, c]])), axis=1)
    n0 = np.arange(32)
    tw = np.stack(turn(n0, i128, 4096, 1)).reshape(2, 8, 4, 1, 128)
    made["tw4"] = np.broadcast_to(tw, (2, 8, 4, 8, 128)).astype(np.float32)
    c, s = turn(n0, n0, 32, 1)
    v4 = np.block([[c, -s], [s, c]]) / 64.0
    made["v4"] = split(np.kron(v4, np.eye(8)))[0]
    return made


def nt(left, right):
    return lax.dot_general(left, right, (((1,), (1,)), ((), ())), preferred_element_type=F32)


def tn(left, right):
    return lax.dot_general(left, right, (((0,), (0,)), ((), ())), preferred_element_type=F32)


def nn(left, right):
    return jnp.dot(left, right, preferred_element_type=F32)


def route_phase(me, tile_ref, cell_ref, w_ref, idx_ref, place_ref):
    tiles = tile_ref[...]
    mine = tile_ref[pl.ds(me, 1), :]
    marks = jnp.concatenate(
        [mine == lax.broadcasted_iota(jnp.int32, (16, 512), 0), tiles == me], axis=0
    ).astype(F32)
    before = lax.broadcasted_iota(jnp.int32, (512, 512), 0) < lax.broadcasted_iota(
        jnp.int32, (512, 512), 1
    )
    rank = nn(marks.astype(BF16), before.astype(F32).astype(BF16))
    rank = jnp.where(marks > 0.5, rank, -1.0).astype(jnp.int32)
    position = lax.broadcasted_iota(jnp.int32, (16, 512), 1)
    columns = [
        jnp.sum(jnp.where(rank[:16] == k, position, 0), axis=1, keepdims=True) for k in range(8)
    ]
    idx_ref[...] = jnp.concatenate(columns + [columns[0]] * 120, axis=1)
    slot = lax.broadcasted_iota(jnp.int32, (8, 512), 0)
    lane = lax.broadcasted_iota(jnp.int32, (8, 256), 1)
    hits = []
    for g in range(16):
        chosen = rank[16 + g : 17 + g] == slot
        cell = jnp.sum(jnp.where(chosen, cell_ref[g : g + 1, :] + 1, 0), axis=1, keepdims=True) - 1
        for part in range(2):
            at = jnp.where(cell < 0, -1, cell + 128 * part)
            hits.append((lane == at).astype(F32))
    onehot = jnp.concatenate(hits, axis=0).astype(BF16)
    place_ref[...] = nt(w_ref[...], onehot).astype(BF16)


def partner(me, dx, d):
    up = (d + 1) // 2
    dz = jnp.where(lax.rem(d, 2) == 1, up, lax.rem(16 - up, 16))
    x, z = me // 16, lax.rem(me, 16)
    to = lax.rem(x + dx, 4) * 16 + lax.rem(z + dz, 16)
    source = lax.rem(x + 4 - dx, 4) * 16 + lax.rem(z + 16 - dz, 16)
    return to, source


def by_row(me, step):
    return partner(me, step // 16, lax.rem(step, 16))


def by_distance(me, step):
    return partner(me, lax.rem(step, 4), step // 4)


def gx_copy(send_ref, recv_ref, send_sem, recv_sem, to, slot):
    return pltpu.make_async_remote_copy(
        src_ref=send_ref.at[to],
        dst_ref=recv_ref.at[slot],
        send_sem=send_sem.at[to],
        recv_sem=recv_sem.at[slot],
        device_id={"gx": to},
        device_id_type=MESH,
    )


def greet(me, grp):
    barrier = pltpu.get_barrier_semaphore()

    def along_gx(step, carry):
        to, _ = by_row(me, step)
        pl.semaphore_signal(barrier, inc=1, device_id={"gx": to}, device_id_type=MESH)
        return carry

    lax.fori_loop(1, 64, along_gx, 0)

    def along_grp(step, carry):
        to = lax.rem(grp + step, 16)
        pl.semaphore_signal(barrier, inc=1, device_id={"grp": to}, device_id_type=MESH)
        return carry

    lax.fori_loop(1, 16, along_grp, 0)


def spectra_phase(four, x_ref, m1_ref, tw_ref, v_ref, z_ref):
    def quad(h, carry):
        four(h)
        cos, sin = tw_ref[0], tw_ref[1]
        for half in range(2):
            first = 4 * h + 2 * half
            y = nn(m1_ref[...], jnp.concatenate([x_ref[first], x_ref[first + 1]], axis=1))
            y = y[:256] + y[256:]
            both = []
            for o in range(2):
                re, im = y[:128, o * 128 : o * 128 + 128], y[128:, o * 128 : o * 128 + 128]
                both.append(jnp.concatenate([re * cos - im * sin, re * sin + im * cos], axis=1))
            both = jnp.concatenate(both, axis=0)
            high = both.astype(BF16)
            low = (both - high.astype(F32)).astype(BF16)
            out = nt(v_ref[...], high)
            out = out[:256] + out[256:] + nt(v_ref[:256], low)
            for o in range(2):
                for s in range(4):
                    z_ref[pl.ds(s * 16 + first + o, 64, stride=64), :] = out[
                        s * 64 : s * 64 + 64, o * 128 : o * 128 + 128
                    ]
        return carry

    lax.fori_loop(0, 4, quad, 0)


def operand(recv_ref, at):
    return jnp.concatenate(
        [recv_ref[pl.ds(at * 16, 16), s * 16 : s * 16 + 16, :].reshape(256, 128) for s in range(4)],
        axis=1,
    )


def gram_block(recv_ref, vis_ref, r, p):
    left, right = operand(recv_ref, r), operand(recv_ref, p)
    crossed = jnp.concatenate([-right[:, 256:], right[:, :256]], axis=1)
    for part, other in enumerate((right, crossed)):
        out = nt(left, other)
        for half in range(2):
            vis_ref[pl.ds(r * 16, 16), 2 * p + half, part * 16 : part * 16 + 16, :] = out[
                :, half * 128 : half * 128 + 128
            ].reshape(16, 16, 128)


def gram_last(recv_ref, vis_ref, new, others):
    right = operand(recv_ref, new)
    crossed = jnp.concatenate([-right[:, 256:], right[:, :256]], axis=1)
    left = jnp.concatenate(
        [recv_ref[:, s * 16 : s * 16 + 16, :].reshape(1024, 128) for s in range(4)], axis=1
    )
    for part, other in enumerate((right, crossed)):
        out = nt(left, other)
        for half in range(2):
            vis_ref[:, 2 * new + half, part * 16 : part * 16 + 16, :] = out[
                :, half * 128 : half * 128 + 128
            ].reshape(64, 16, 128)
    for p in others:
        gram_block(recv_ref, vis_ref, new, p)


def gather_phase(u, idx_ref, vis_ref, z_ref, out_ref):
    def tile(t, carry):
        for k in range(8):
            b = idx_ref[t, k]
            block = vis_ref[b // 8, lax.rem(b, 8)]
            for part in range(2):
                z_ref[pl.ds(t * 64 + part * 8 + k, 4, stride=16), :] = block[
                    part * 16 + u * 4 : part * 16 + u * 4 + 4
                ]
        out_ref[t, u * 64 : u * 64 + 64, :] = (z_ref[pl.ds(t * 64, 64), :] * 0.0625).astype(BF16)
        return carry

    lax.fori_loop(0, 16, tile, 0, unroll=2)


def rows_phase(u, units, local, got_ref, place_ref, tw_ref, v_ref, y_ref, z_ref):
    cos, sin = tw_ref[0], tw_ref[1]
    for i in (0, 2):
        row = (u * 4 + i) * 16
        pair = [got_ref[:, row + o * 16 : row + o * 16 + 16, :].reshape(256, 128) for o in range(2)]
        y = nn(place_ref[...], jnp.concatenate(pair, axis=1))
        y = y[:256] + y[256:]
        for o in range(2):
            re, im = y[:128, o * 128 : o * 128 + 128], y[128:, o * 128 : o * 128 + 128]
            at = slice((i + o) * 32, (i + o) * 32 + 32)
            y_ref[:, at, 0:128] = (re * cos - im * sin).astype(BF16).reshape(4, 32, 128)
            y_ref[:, at, 128:256] = (re * sin + im * cos).astype(BF16).reshape(4, 32, 128)
    for m in (0, 2):
        out = nt(v_ref[...], y_ref[m : m + 2].reshape(256, 256))
        for o in range(2):
            for s in range(4):
                z_ref[pl.ds(local * 16 + (m + o) * 4 + s, 64, stride=16 * units), :] = out[
                    s * 64 : s * 64 + 64, o * 128 : o * 128 + 128
                ]


PARTS = ((0, 1), (1, 1), (2, 2))


def main_kernel(
    x_hbm, tile_hbm, cell_hbm, m1_hbm, tw1_hbm, v1_hbm, w_hbm, tw2_hbm, v2_hbm, out_ref,
    x_ref, tile_ref, cell_ref, m1_ref, tw1_ref, v1_ref, w_ref, tw2_ref, v2_ref,
    z_ref, vis_ref, send_ref, recv_ref, idx_ref, pick_ref, place_ref, blocks_ref, got_ref, y_ref, turned_ref,
    rsend_ref, rrecv_ref, load_sem, four_sem, send_sem, recv_sem, pick_sem, bsend_sem, brecv_sem, rsend_sem, rrecv_sem,
):
    me, grp = lax.axis_index("gx"), lax.axis_index("grp")
    loads = [
        pltpu.make_async_copy(source, target, load_sem.at[n])
        for n, (source, target) in enumerate(
            (
                (m1_hbm, m1_ref), (tw1_hbm, tw1_ref), (v1_hbm, v1_ref), (tile_hbm, tile_ref),
                (cell_hbm, cell_ref), (w_hbm, w_ref), (tw2_hbm, tw2_ref), (v2_hbm, v2_ref),
            )
        )
    ]

    def load_four(h):
        at = pl.ds(h * 4, 4)
        return pltpu.make_async_copy(x_hbm.at[at], x_ref.at[at], four_sem.at[h])

    loads[0].start()
    load_four(0).start()
    loads[1].start()
    loads[2].start()
    for h in range(1, 4):
        load_four(h).start()
    for load in loads[3:]:
        load.start()
    greet(me, grp)
    for load in loads[:3]:
        load.wait()
    spectra_phase(lambda h: load_four(h).wait(), x_ref, m1_ref, tw1_ref, v1_ref, z_ref)
    pl.semaphore_wait(pltpu.get_barrier_semaphore(), 78)

    def push(step, carry):
        to, _ = by_row(me, step)
        send_ref[to] = z_ref[pl.ds(pl.multiple_of(to * 64, 64), 64), :].astype(BF16)
        gx_copy(send_ref, recv_ref, send_sem, recv_sem, to, me).start()
        return carry

    lax.fori_loop(1, 64, push, 0)
    recv_ref[me] = z_ref[pl.ds(pl.multiple_of(me * 64, 64), 64), :].astype(BF16)

    for load in loads[3:]:
        load.wait()
    route_phase(grp, tile_ref, cell_ref, w_ref, idx_ref, place_ref)
    picks = pltpu.make_async_copy(idx_ref, pick_ref, pick_sem)
    picks.start()
    picks.wait()

    def take(step, carry):
        to, source = by_row(me, step)
        gx_copy(send_ref, recv_ref, send_sem, recv_sem, to, source).wait()
        return carry

    row = me // 16
    groups = [lax.rem(row + 4 - dx, 4) for dx in range(4)]
    for dx in range(4):
        lax.fori_loop(max(1, 16 * dx), 16 * dx + 16, take, 0)
        if dx == 3:
            break

        def against(j, carry, dx=dx):
            gram_block(recv_ref, vis_ref, groups[dx], lax.rem(row + 4 - j, 4))
            return carry

        def under(j, carry, dx=dx):
            gram_block(recv_ref, vis_ref, lax.rem(row + 4 - j, 4), groups[dx])
            return carry

        lax.fori_loop(0, dx + 1, against, 0)
        if dx:
            lax.fori_loop(0, dx, under, 0)
    gram_last(recv_ref, vis_ref, groups[3], groups[:3])

    def block_copy(p, to, slot):
        at = pl.ds(PARTS[p][0] * 64, PARTS[p][1] * 64)
        return pltpu.make_async_remote_copy(
            src_ref=blocks_ref.at[to, at],
            dst_ref=got_ref.at[slot, at],
            send_sem=bsend_sem.at[p, to],
            recv_sem=brecv_sem.at[p, slot],
            device_id={"grp": to},
            device_id_type=MESH,
        )

    def push_blocks(p):
        def one(step, carry):
            block_copy(p, lax.rem(grp + step, 16), grp).start()
            return carry

        lax.fori_loop(1, 16, one, 0)
        at = slice(PARTS[p][0] * 64, sum(PARTS[p]) * 64)
        got_ref[grp, at, :] = blocks_ref[grp, at, :]

    def take_blocks(p):
        def one(step, carry):
            block_copy(p, lax.rem(grp + step, 16), lax.rem(grp + 16 - step, 16)).wait()
            return carry

        lax.fori_loop(1, 16, one, 0)

    def row_copy(p, to, slot):
        at = pl.ds(PARTS[p][0] * 16, PARTS[p][1] * 16)
        return pltpu.make_async_remote_copy(
            src_ref=rsend_ref.at[to, at],
            dst_ref=rrecv_ref.at[slot, at],
            send_sem=rsend_sem.at[p, to],
            recv_sem=rrecv_sem.at[p, slot],
            device_id={"gx": to},
            device_id_type=MESH,
        )

    def rows(p):
        first, units = PARTS[p]
        for local in range(units):
            rows_phase(first + local, units, local, got_ref, place_ref, tw2_ref, v2_ref, y_ref, z_ref)

    def push_rows(p):
        first, units = PARTS[p]
        n = units * 16

        def one(step, carry):
            to, _ = by_distance(me, step)
            rsend_ref[to, first * 16 : first * 16 + n, :] = z_ref[
                pl.ds(pl.multiple_of(to * n, n), n), :
            ].astype(BF16)
            row_copy(p, to, me).start()
            return carry

        lax.fori_loop(1, 64, one, 0)
        own = z_ref[pl.ds(pl.multiple_of(me * n, n), n), :].astype(BF16)
        turned_ref[pl.ds(first * 1024 + me, n, stride=64), :] = own.astype(F32)

    def take_rows(p):
        first, units = PARTS[p]
        n = units * 16

        def one(step, carry):
            to, source = by_distance(me, step)
            row_copy(p, to, source).wait()
            turned_ref[pl.ds(first * 1024 + source, n, stride=64), :] = rrecv_ref[
                source, first * 16 : first * 16 + n, :
            ].astype(F32)
            return carry

        lax.fori_loop(1, 64, one, 0)
        at = slice(first * 1024, (first + units) * 1024)
        out_ref[at, :] = turned_ref[at, :].astype(BF16)

    gather_phase(0, pick_ref, vis_ref, z_ref, blocks_ref)
    push_blocks(0)
    for u in range(1, 4):
        gather_phase(u, pick_ref, vis_ref, z_ref, blocks_ref)
    take_blocks(0)
    push_blocks(1)
    push_blocks(2)
    for p in range(3):
        if p:
            take_blocks(p)
        rows(p)
        push_rows(p)
    for p in range(3):
        take_rows(p)


def columns_kernel(x_ref, m4_ref, tw_ref, v_ref, image_ref):
    k2 = pl.program_id(0)
    turned = []
    for n in range(2):
        for u in range(4):
            x = jnp.concatenate(
                [
                    x_ref[u * 16 + (2 * bit + n) * 4 + part * 2 + k2]
                    for part in range(2)
                    for bit in range(2)
                ],
                axis=0,
            )
            t = tn(x, m4_ref[...])
            t = t[:, :256] + t[:, 256:]
            re, im = (t[:, o * 128 : o * 128 + 128].reshape(4, 4, 8, 128) for o in range(2))
            cos, sin = (tw_ref[o, n * 4 + u].reshape(4, 1, 8, 128) for o in range(2))
            turned.append((re * cos - im * sin, re * sin + im * cos))
    for pair in (0, 2):
        sides = [
            jnp.concatenate(
                [turned[nu][part][:, side].reshape(32, 128) for part in range(2) for nu in range(8)],
                axis=0,
            )
            for side in (pair, pair + 1)
        ]
        out = nn(v_ref[...], jnp.concatenate(sides, axis=1).astype(BF16))
        for part in range(2):
            for k in range(32):
                for o in range(2):
                    at = (pair + o) * 8
                    image_ref[part, at : at + 8, k * 128 : k * 128 + 128] = out[
                        (part * 32 + k) * 8 : (part * 32 + k) * 8 + 8, o * 128 : o * 128 + 128
                    ]


def params(mib, **more):
    return pltpu.CompilerParams(vmem_limit_bytes=mib * 1024 * 1024, **more)


def on_device(voltages, tile_of, cell_of):
    tab = {name: jnp.asarray(value) for name, value in tables().items()}
    vmem = pl.BlockSpec(memory_space=pltpu.VMEM)
    volts = voltages.reshape(16, 2, 128, 128).transpose(0, 2, 1, 3).reshape(16, 256, 128)
    columns = pl.pallas_call(
        main_kernel,
        out_shape=jax.ShapeDtypeStruct((4096, 128), BF16),
        in_specs=[pl.BlockSpec(memory_space=pltpu.HBM)] * 9,
        out_specs=vmem,
        scratch_shapes=[
            pltpu.VMEM((16, 256, 128), BF16),
            pltpu.VMEM((16, 512), jnp.int32),
            pltpu.VMEM((16, 512), jnp.int32),
            *(pltpu.VMEM(tab[name].shape, tab[name].dtype) for name in ("m1", "tw1", "v1", "w", "tw2", "v2")),
            pltpu.VMEM((4096, 128), F32),
            pltpu.VMEM((64, 8, 32, 128), F32),
            pltpu.VMEM((64, 64, 128), BF16),
            pltpu.VMEM((64, 64, 128), BF16),
            pltpu.VMEM((16, 128), jnp.int32),
            pltpu.SMEM((16, 128), jnp.int32),
            pltpu.VMEM((512, 256), BF16),
            pltpu.VMEM((16, 256, 128), BF16),
            pltpu.VMEM((16, 256, 128), BF16),
            pltpu.VMEM((4, 128, 256), BF16),
            pltpu.VMEM((4096, 128), F32),
            pltpu.VMEM((64, 64, 128), BF16),
            pltpu.VMEM((64, 64, 128), BF16),
            pltpu.SemaphoreType.DMA((8,)),
            pltpu.SemaphoreType.DMA((4,)),
            pltpu.SemaphoreType.DMA((64,)),
            pltpu.SemaphoreType.DMA((64,)),
            pltpu.SemaphoreType.DMA,
            pltpu.SemaphoreType.DMA((3, 16)),
            pltpu.SemaphoreType.DMA((3, 16)),
            pltpu.SemaphoreType.DMA((3, 64)),
            pltpu.SemaphoreType.DMA((3, 64)),
        ],
        compiler_params=params(40, collective_id=0, has_side_effects=True),
        name="main",
    )(
        *(
            pltpu.with_memory_space_constraint(array, pltpu.HBM)
            for array in (
                volts, tile_of, cell_of, tab["m1"], tab["tw1"], tab["v1"], tab["w"], tab["tw2"], tab["v2"]
            )
        )
    )
    whole = lambda shape: pl.BlockSpec(shape, lambda e: (0,) * len(shape))
    image = pl.pallas_call(
        columns_kernel,
        grid=(2,),
        out_shape=jax.ShapeDtypeStruct((2, 64, 4096), F32),
        in_specs=[whole(s) for s in ((64, 64, 128), tab["m4"].shape, tab["tw4"].shape, tab["v4"].shape)],
        out_specs=pl.BlockSpec((2, 32, 4096), lambda e: (0, e, 0)),
        compiler_params=params(20),
        name="columns",
    )(columns.reshape(64, 64, 128), tab["m4"], tab["tw4"], tab["v4"])
    return image.reshape(1, 2, 64, 4096)


def solution(mesh):
    in_specs = (P("grp", "gx", None, None, None, None), P(None, "gx"), P(None, "gx"))
    out_specs = P("grp", None, "gx", None)
    return jax.shard_map(
        on_device, mesh=mesh, in_specs=in_specs, out_specs=out_specs, check_vma=False
    )
```

```python
import functools
import math

import jax
import jax.numpy as jnp
import numpy as np
from jax import lax
from jax.experimental import pallas as pl
from jax.experimental.pallas import tpu as pltpu
from jax.sharding import PartitionSpec as P

F32 = jnp.float32
BF16 = jnp.bfloat16
MESH = pl.DeviceIdType.MESH


def split(table):
    high = table.astype(np.float32).astype(jnp.bfloat16)
    low = (table - high.astype(np.float64)).astype(np.float32).astype(jnp.bfloat16)
    return high, low


def turn(left, right, size, sign):
    angle = sign * 2.0 * math.pi / size * (np.outer(left, right) % size)
    return np.cos(angle), np.sin(angle)


@functools.cache
def tables():
    made = {}
    i128 = np.arange(128)
    c, s = turn(i128, i128, 128, -1)
    m1 = np.zeros((2, 128, 128, 2))
    m1[0, :, :, 0], m1[0, :, :, 1] = c, -s
    m1[1, :, :, 0], m1[1, :, :, 1] = s, c
    made["m1"] = np.concatenate(split(m1.reshape(256, 256)))
    made["tw1"] = np.stack(turn(i128, i128, 16384, -1)).astype(np.float32)
    c, s = turn(i128, i128, 128, -1)
    c, s = (t.reshape(64, 2, 128).transpose(1, 0, 2).reshape(128, 128) / 128.0 for t in (c, s))
    made["v1"] = np.concatenate(split(np.block([[c, -s], [s, c]])))
    c, s = turn(np.arange(32), np.arange(32), 32, 1)
    w = np.zeros((2, 4, 32, 2, 4, 32))
    for rb in range(4):
        w[0, rb, :, 0, rb], w[0, rb, :, 1, rb] = c, -s
        w[1, rb, :, 0, rb], w[1, rb, :, 1, rb] = s, c
    made["w"] = np.concatenate(split(w.reshape(256, 256)))
    tw = np.stack(turn(np.arange(32), i128, 4096, 1))
    made["tw2"] = np.tile(tw, (1, 4, 1)).astype(np.float32)
    c, s = turn(i128, i128, 128, 1)
    c, s = (t.reshape(64, 2, 128).transpose(1, 0, 2).reshape(128, 128) / 64.0 for t in (c, s))
    made["v2"] = split(np.block([[c, -s], [s, c]]))[0]
    n1 = (2 * np.arange(64)[None, :] + np.arange(2)[:, None]).reshape(128)
    c, s = turn(n1, i128, 128, 1)
    made["m4"] = np.concatenate(split(np.block([[c, s], [-s, c]])), axis=1)
    n0 = np.arange(32)
    tw = np.stack(turn(n0, i128, 4096, 1)).reshape(2, 8, 4, 1, 128)
    made["tw4"] = np.broadcast_to(tw, (2, 8, 4, 8, 128)).astype(np.float32)
    c, s = turn(n0, n0, 32, 1)
    v4 = np.block([[c, -s], [s, c]]) / 64.0
    made["v4"] = split(np.kron(v4, np.eye(8)))[0]
    return made


def nt(left, right):
    return lax.dot_general(left, right, (((1,), (1,)), ((), ())), preferred_element_type=F32)


def tn(left, right):
    return lax.dot_general(left, right, (((0,), (0,)), ((), ())), preferred_element_type=F32)


def nn(left, right):
    return jnp.dot(left, right, preferred_element_type=F32)


def route_phase(me, tile_ref, cell_ref, w_ref, idx_ref, place_ref):
    tiles = tile_ref[...]
    mine = tile_ref[pl.ds(me, 1), :]
    marks = jnp.concatenate(
        [mine == lax.broadcasted_iota(jnp.int32, (16, 512), 0), tiles == me], axis=0
    ).astype(F32)
    before = lax.broadcasted_iota(jnp.int32, (512, 512), 0) < lax.broadcasted_iota(
        jnp.int32, (512, 512), 1
    )
    rank = nn(marks.astype(BF16), before.astype(F32).astype(BF16))
    rank = jnp.where(marks > 0.5, rank, -1.0).astype(jnp.int32)
    position = lax.broadcasted_iota(jnp.int32, (16, 512), 1)
    columns = [
        jnp.sum(jnp.where(rank[:16] == k, position, 0), axis=1, keepdims=True) for k in range(8)
    ]
    idx_ref[...] = jnp.concatenate(columns + [columns[0]] * 120, axis=1)
    slot = lax.broadcasted_iota(jnp.int32, (8, 512), 0)
    lane = lax.broadcasted_iota(jnp.int32, (8, 256), 1)
    hits = []
    for g in range(16):
        chosen = rank[16 + g : 17 + g] == slot
        cell = jnp.sum(jnp.where(chosen, cell_ref[g : g + 1, :] + 1, 0), axis=1, keepdims=True) - 1
        for part in range(2):
            at = jnp.where(cell < 0, -1, cell + 128 * part)
            hits.append((lane == at).astype(F32))
    onehot = jnp.concatenate(hits, axis=0).astype(BF16)
    place_ref[...] = nt(w_ref[...], onehot).astype(BF16)


def partner(me, dx, d):
    up = (d + 1) // 2
    dz = jnp.where(lax.rem(d, 2) == 1, up, lax.rem(16 - up, 16))
    x, z = me // 16, lax.rem(me, 16)
    to = lax.rem(x + dx, 4) * 16 + lax.rem(z + dz, 16)
    source = lax.rem(x + 4 - dx, 4) * 16 + lax.rem(z + 16 - dz, 16)
    return to, source


def by_row(me, step):
    return partner(me, step // 16, lax.rem(step, 16))


def by_distance(me, step):
    return partner(me, lax.rem(step, 4), step // 4)


def by_start(me, step):
    dx = lax.rem(step, 4)
    d = step // 4
    z = lax.rem(me, 16)
    i = d // 2
    wrapped = jnp.maximum(z - 7, 0)
    up = jnp.where(i < wrapped, i, z + 1 + i - wrapped)
    low = jnp.maximum(z - 7, 0)
    j = i - 1
    down = jnp.where(j < z - low, low + j, z + 9 + j - (z - low))
    zt = jnp.where(lax.rem(d, 2) == 1, up, jnp.where(d == 0, z, down))
    return lax.rem(me // 16 + dx, 4) * 16 + zt


def gx_copy(send_ref, recv_ref, send_sem, recv_sem, to, slot):
    return pltpu.make_async_remote_copy(
        src_ref=send_ref.at[to],
        dst_ref=recv_ref.at[slot],
        send_sem=send_sem.at[to],
        recv_sem=recv_sem.at[slot],
        device_id={"gx": to},
        device_id_type=MESH,
    )


def greet(me, grp):
    barrier = pltpu.get_barrier_semaphore()

    def along_gx(step, carry):
        to, _ = by_row(me, step)
        pl.semaphore_signal(barrier, inc=1, device_id={"gx": to}, device_id_type=MESH)
        return carry

    lax.fori_loop(1, 64, along_gx, 0)

    def along_grp(step, carry):
        to = lax.rem(grp + step, 16)
        pl.semaphore_signal(barrier, inc=1, device_id={"grp": to}, device_id_type=MESH)
        return carry

    lax.fori_loop(1, 16, along_grp, 0)


def spectra_phase(four, x_ref, m1_ref, tw_ref, v_ref, z_ref):
    def quad(h, carry):
        four(h)
        cos, sin = tw_ref[0], tw_ref[1]
        for half in range(2):
            first = 4 * h + 2 * half
            y = nn(m1_ref[...], jnp.concatenate([x_ref[first], x_ref[first + 1]], axis=1))
            y = y[:256] + y[256:]
            both = []
            for o in range(2):
                re, im = y[:128, o * 128 : o * 128 + 128], y[128:, o * 128 : o * 128 + 128]
                both.append(jnp.concatenate([re * cos - im * sin, re * sin + im * cos], axis=1))
            both = jnp.concatenate(both, axis=0)
            high = both.astype(BF16)
            low = (both - high.astype(F32)).astype(BF16)
            out = nt(v_ref[...], high)
            out = out[:256] + out[256:] + nt(v_ref[:256], low)
            for o in range(2):
                for s in range(4):
                    z_ref[pl.ds(s * 16 + first + o, 64, stride=64), :] = out[
                        s * 64 : s * 64 + 64, o * 128 : o * 128 + 128
                    ]
        return carry

    lax.fori_loop(0, 4, quad, 0)


def operand(recv_ref, at):
    return jnp.concatenate(
        [recv_ref[pl.ds(at * 16, 16), s * 16 : s * 16 + 16, :].reshape(256, 128) for s in range(4)],
        axis=1,
    )


def gram_block(recv_ref, vis_ref, r, p):
    left, right = operand(recv_ref, r), operand(recv_ref, p)
    crossed = jnp.concatenate([-right[:, 256:], right[:, :256]], axis=1)
    for part, other in enumerate((right, crossed)):
        out = nt(left, other)
        for half in range(2):
            vis_ref[pl.ds(r * 16, 16), 2 * p + half, part * 16 : part * 16 + 16, :] = out[
                :, half * 128 : half * 128 + 128
            ].reshape(16, 16, 128)


def gram_last(recv_ref, vis_ref, new, others):
    right = operand(recv_ref, new)
    crossed = jnp.concatenate([-right[:, 256:], right[:, :256]], axis=1)
    left = jnp.concatenate(
        [recv_ref[:, s * 16 : s * 16 + 16, :].reshape(1024, 128) for s in range(4)], axis=1
    )
    for part, other in enumerate((right, crossed)):
        out = nt(left, other)
        for half in range(2):
            vis_ref[:, 2 * new + half, part * 16 : part * 16 + 16, :] = out[
                :, half * 128 : half * 128 + 128
            ].reshape(64, 16, 128)
    for p in others:
        gram_block(recv_ref, vis_ref, new, p)


def gather_phase(u, idx_ref, vis_ref, z_ref, out_ref):
    def tile(t, carry):
        for k in range(8):
            b = idx_ref[t, k]
            block = vis_ref[b // 8, lax.rem(b, 8)]
            for part in range(2):
                z_ref[pl.ds(t * 64 + part * 8 + k, 4, stride=16), :] = block[
                    part * 16 + u * 4 : part * 16 + u * 4 + 4
                ]
        out_ref[t, u * 64 : u * 64 + 64, :] = (z_ref[pl.ds(t * 64, 64), :] * 0.0625).astype(BF16)
        return carry

    lax.fori_loop(0, 16, tile, 0, unroll=2)


def rows_phase(u, units, local, got_ref, place_ref, tw_ref, v_ref, y_ref, z_ref):
    cos, sin = tw_ref[0], tw_ref[1]
    for i in (0, 2):
        row = (u * 4 + i) * 16
        pair = [got_ref[:, row + o * 16 : row + o * 16 + 16, :].reshape(256, 128) for o in range(2)]
        y = nn(place_ref[...], jnp.concatenate(pair, axis=1))
        y = y[:256] + y[256:]
        for o in range(2):
            re, im = y[:128, o * 128 : o * 128 + 128], y[128:, o * 128 : o * 128 + 128]
            at = slice((i + o) * 32, (i + o) * 32 + 32)
            y_ref[:, at, 0:128] = (re * cos - im * sin).astype(BF16).reshape(4, 32, 128)
            y_ref[:, at, 128:256] = (re * sin + im * cos).astype(BF16).reshape(4, 32, 128)
    for m in (0, 2):
        out = nt(v_ref[...], y_ref[m : m + 2].reshape(256, 256))
        for o in range(2):
            for s in range(4):
                z_ref[pl.ds(local * 16 + (m + o) * 4 + s, 64, stride=16 * units), :] = out[
                    s * 64 : s * 64 + 64, o * 128 : o * 128 + 128
                ]


PARTS = ((0, 2), (2, 2))


def main_kernel(
    x_hbm, tile_hbm, cell_hbm, m1_hbm, tw1_hbm, v1_hbm, w_hbm, tw2_hbm, v2_hbm, out_ref,
    x_ref, tile_ref, cell_ref, m1_ref, tw1_ref, v1_ref, w_ref, tw2_ref, v2_ref,
    z_ref, vis_ref, send_ref, recv_ref, idx_ref, pick_ref, place_ref, blocks_ref, got_ref, y_ref, turned_ref,
    rsend_ref, rrecv_ref, load_sem, four_sem, send_sem, recv_sem, pick_sem, bsend_sem, brecv_sem, rsend_sem, rrecv_sem,
):
    me, grp = lax.axis_index("gx"), lax.axis_index("grp")
    loads = [
        pltpu.make_async_copy(source, target, load_sem.at[n])
        for n, (source, target) in enumerate(
            (
                (m1_hbm, m1_ref), (tw1_hbm, tw1_ref), (v1_hbm, v1_ref), (tile_hbm, tile_ref),
                (cell_hbm, cell_ref), (w_hbm, w_ref), (tw2_hbm, tw2_ref), (v2_hbm, v2_ref),
            )
        )
    ]

    def load_four(h):
        at = pl.ds(h * 4, 4)
        return pltpu.make_async_copy(x_hbm.at[at], x_ref.at[at], four_sem.at[h])

    loads[0].start()
    load_four(0).start()
    loads[1].start()
    loads[2].start()
    for h in range(1, 4):
        load_four(h).start()
    for load in loads[3:]:
        load.start()
    greet(me, grp)
    for load in loads[:3]:
        load.wait()
    spectra_phase(lambda h: load_four(h).wait(), x_ref, m1_ref, tw1_ref, v1_ref, z_ref)
    pl.semaphore_wait(pltpu.get_barrier_semaphore(), 78)

    def push(step, carry):
        to, _ = by_row(me, step)
        send_ref[to] = z_ref[pl.ds(pl.multiple_of(to * 64, 64), 64), :].astype(BF16)
        gx_copy(send_ref, recv_ref, send_sem, recv_sem, to, me).start()
        return carry

    lax.fori_loop(1, 64, push, 0)
    recv_ref[me] = z_ref[pl.ds(pl.multiple_of(me * 64, 64), 64), :].astype(BF16)

    for load in loads[3:]:
        load.wait()
    route_phase(grp, tile_ref, cell_ref, w_ref, idx_ref, place_ref)
    picks = pltpu.make_async_copy(idx_ref, pick_ref, pick_sem)
    picks.start()
    picks.wait()

    def take(step, carry):
        to, source = by_row(me, step)
        gx_copy(send_ref, recv_ref, send_sem, recv_sem, to, source).wait()
        return carry

    row = me // 16
    groups = [lax.rem(row + 4 - dx, 4) for dx in range(4)]
    for dx in range(4):
        lax.fori_loop(max(1, 16 * dx), 16 * dx + 16, take, 0)
        if dx == 3:
            break

        def against(j, carry, dx=dx):
            gram_block(recv_ref, vis_ref, groups[dx], lax.rem(row + 4 - j, 4))
            return carry

        def under(j, carry, dx=dx):
            gram_block(recv_ref, vis_ref, lax.rem(row + 4 - j, 4), groups[dx])
            return carry

        lax.fori_loop(0, dx + 1, against, 0)
        if dx:
            lax.fori_loop(0, dx, under, 0)
    gram_last(recv_ref, vis_ref, groups[3], groups[:3])

    def block_copy(p, to, slot):
        at = pl.ds(PARTS[p][0] * 64, PARTS[p][1] * 64)
        return pltpu.make_async_remote_copy(
            src_ref=blocks_ref.at[to, at],
            dst_ref=got_ref.at[slot, at],
            send_sem=bsend_sem.at[p, to],
            recv_sem=brecv_sem.at[p, slot],
            device_id={"grp": to},
            device_id_type=MESH,
        )

    def push_blocks(p):
        def one(step, carry):
            block_copy(p, lax.rem(grp + step, 16), grp).start()
            return carry

        lax.fori_loop(1, 16, one, 0)
        at = slice(PARTS[p][0] * 64, sum(PARTS[p]) * 64)
        got_ref[grp, at, :] = blocks_ref[grp, at, :]

    def take_blocks(p):
        def one(step, carry):
            block_copy(p, lax.rem(grp + step, 16), lax.rem(grp + 16 - step, 16)).wait()
            return carry

        lax.fori_loop(1, 16, one, 0)

    def row_copy(p, to, slot):
        at = pl.ds(PARTS[p][0] * 16, PARTS[p][1] * 16)
        return pltpu.make_async_remote_copy(
            src_ref=rsend_ref.at[to, at],
            dst_ref=rrecv_ref.at[slot, at],
            send_sem=rsend_sem.at[p, to],
            recv_sem=rrecv_sem.at[p, slot],
            device_id={"gx": to},
            device_id_type=MESH,
        )

    def rows(p):
        first, units = PARTS[p]
        for local in range(units):
            rows_phase(first + local, units, local, got_ref, place_ref, tw2_ref, v2_ref, y_ref, z_ref)

    def push_rows(p):
        first, units = PARTS[p]
        n = units * 16

        def one(step, carry):
            to = by_start(me, step)
            rsend_ref[to, first * 16 : first * 16 + n, :] = z_ref[
                pl.ds(pl.multiple_of(to * n, n), n), :
            ].astype(BF16)
            row_copy(p, to, me).start()
            return carry

        lax.fori_loop(1, 64, one, 0)
        own = z_ref[pl.ds(pl.multiple_of(me * n, n), n), :].astype(BF16)
        turned_ref[pl.ds(first * 1024 + me, n, stride=64), :] = own.astype(F32)

    def take_rows(p):
        first, units = PARTS[p]
        n = units * 16

        def one(step, carry):
            to, source = by_distance(me, step)
            row_copy(p, to, source).wait()
            turned_ref[pl.ds(first * 1024 + source, n, stride=64), :] = rrecv_ref[
                source, first * 16 : first * 16 + n, :
            ].astype(F32)
            return carry

        lax.fori_loop(1, 64, one, 0)
        at = slice(first * 1024, (first + units) * 1024)
        out_ref[at, :] = turned_ref[at, :].astype(BF16)

    for u in range(2):
        gather_phase(u, pick_ref, vis_ref, z_ref, blocks_ref)
    push_blocks(0)
    for u in range(2, 4):
        gather_phase(u, pick_ref, vis_ref, z_ref, blocks_ref)
    take_blocks(0)
    push_blocks(1)
    for p in range(2):
        if p:
            take_blocks(p)
        rows(p)
        push_rows(p)
    for p in range(2):
        take_rows(p)


def columns_kernel(x_ref, m4_ref, tw_ref, v_ref, image_ref):
    k2 = pl.program_id(0)
    turned = []
    for n in range(2):
        for u in range(4):
            x = jnp.concatenate(
                [
                    x_ref[u * 16 + (2 * bit + n) * 4 + part * 2 + k2]
                    for part in range(2)
                    for bit in range(2)
                ],
                axis=0,
            )
            t = tn(x, m4_ref[...])
            t = t[:, :256] + t[:, 256:]
            re, im = (t[:, o * 128 : o * 128 + 128].reshape(4, 4, 8, 128) for o in range(2))
            cos, sin = (tw_ref[o, n * 4 + u].reshape(4, 1, 8, 128) for o in range(2))
            turned.append((re * cos - im * sin, re * sin + im * cos))
    for pair in (0, 2):
        sides = [
            jnp.concatenate(
                [turned[nu][part][:, side].reshape(32, 128) for part in range(2) for nu in range(8)],
                axis=0,
            )
            for side in (pair, pair + 1)
        ]
        out = nn(v_ref[...], jnp.concatenate(sides, axis=1).astype(BF16))
        for part in range(2):
            for k in range(32):
                for o in range(2):
                    at = (pair + o) * 8
                    image_ref[part, at : at + 8, k * 128 : k * 128 + 128] = out[
                        (part * 32 + k) * 8 : (part * 32 + k) * 8 + 8, o * 128 : o * 128 + 128
                    ]


def params(mib, **more):
    return pltpu.CompilerParams(vmem_limit_bytes=mib * 1024 * 1024, **more)


def on_device(voltages, tile_of, cell_of):
    tab = {name: jnp.asarray(value) for name, value in tables().items()}
    vmem = pl.BlockSpec(memory_space=pltpu.VMEM)
    volts = voltages.reshape(16, 2, 128, 128).transpose(0, 2, 1, 3).reshape(16, 256, 128)
    columns = pl.pallas_call(
        main_kernel,
        out_shape=jax.ShapeDtypeStruct((4096, 128), BF16),
        in_specs=[pl.BlockSpec(memory_space=pltpu.HBM)] * 9,
        out_specs=vmem,
        scratch_shapes=[
            pltpu.VMEM((16, 256, 128), BF16),
            pltpu.VMEM((16, 512), jnp.int32),
            pltpu.VMEM((16, 512), jnp.int32),
            *(pltpu.VMEM(tab[name].shape, tab[name].dtype) for name in ("m1", "tw1", "v1", "w", "tw2", "v2")),
            pltpu.VMEM((4096, 128), F32),
            pltpu.VMEM((64, 8, 32, 128), F32),
            pltpu.VMEM((64, 64, 128), BF16),
            pltpu.VMEM((64, 64, 128), BF16),
            pltpu.VMEM((16, 128), jnp.int32),
            pltpu.SMEM((16, 128), jnp.int32),
            pltpu.VMEM((512, 256), BF16),
            pltpu.VMEM((16, 256, 128), BF16),
            pltpu.VMEM((16, 256, 128), BF16),
            pltpu.VMEM((4, 128, 256), BF16),
            pltpu.VMEM((4096, 128), F32),
            pltpu.VMEM((64, 64, 128), BF16),
            pltpu.VMEM((64, 64, 128), BF16),
            pltpu.SemaphoreType.DMA((8,)),
            pltpu.SemaphoreType.DMA((4,)),
            pltpu.SemaphoreType.DMA((64,)),
            pltpu.SemaphoreType.DMA((64,)),
            pltpu.SemaphoreType.DMA,
            pltpu.SemaphoreType.DMA((2, 16)),
            pltpu.SemaphoreType.DMA((2, 16)),
            pltpu.SemaphoreType.DMA((2, 64)),
            pltpu.SemaphoreType.DMA((2, 64)),
        ],
        compiler_params=params(40, collective_id=0, has_side_effects=True),
        name="main",
    )(
        *(
            pltpu.with_memory_space_constraint(array, pltpu.HBM)
            for array in (
                volts, tile_of, cell_of, tab["m1"], tab["tw1"], tab["v1"], tab["w"], tab["tw2"], tab["v2"]
            )
        )
    )
    whole = lambda shape: pl.BlockSpec(shape, lambda e: (0,) * len(shape))
    image = pl.pallas_call(
        columns_kernel,
        grid=(2,),
        out_shape=jax.ShapeDtypeStruct((2, 64, 4096), F32),
        in_specs=[whole(s) for s in ((64, 64, 128), tab["m4"].shape, tab["tw4"].shape, tab["v4"].shape)],
        out_specs=pl.BlockSpec((2, 32, 4096), lambda e: (0, e, 0)),
        compiler_params=params(20),
        name="columns",
    )(columns.reshape(64, 64, 128), tab["m4"], tab["tw4"], tab["v4"])
    return image.reshape(1, 2, 64, 4096)


def solution(mesh):
    in_specs = (P("grp", "gx", None, None, None, None), P(None, "gx"), P(None, "gx"))
    out_specs = P("grp", None, "gx", None)
    return jax.shard_map(
        on_device, mesh=mesh, in_specs=in_specs, out_specs=out_specs, check_vma=False
    )
```
